32 devices in a mesh: row: 4 (over z), col: 4 (over x, core), rep: 2 (over y).
Axes of the slice: x: 2, y: 2, z: 4, core: 2. Of those that a mesh axis runs over, the one named last changes fastest.
Arguments:
- density_blocks: bfloat16 [4, 16, 128, 256], P('row', ('col', 'rep')), may hold values from -1 to 1
- density_columns: int32 [4, 16, 2], P('row', ('col', 'rep')), may hold values from 0 to 3, as said below
- square_pattern: int32 [4, 16, 2], P('row', ('col', 'rep')), may hold values from 0 to 3
- cube_pattern: int32 [4, 16, 2], P('row', ('col', 'rep')), may hold values from 0 to 3
Outputs:
- purified: float32 [4, 16, 128, 256], P('row', ('col', 'rep'))
The draws below stay inside these ranges and needn't reach their ends.
Inputs may be any that keep to these rules, and one draw needn't show every extreme that they name: `density_columns`: the 2 block columns of one block row within one tile are all different.
All inputs are finite; a program needn't handle non-finite values.
Results may differ from the reference program's by a relative error of at most 0.0029.
Values may be sent and summed in bfloat16 or wider, within the bound.
A program may use at most 64 MiB of HBM per device.

```python
import jax
import jax.numpy as jnp
from jax import lax

BLOCK = 128
BR = 4
P_SIZE = 2
Q = 2
NBLK = 16
N_ROW = 4


def draw_density_columns(key, part):
    scores = jax.random.randint(key, (N_ROW, NBLK, BR), 0, 1048576, dtype=jnp.int32)
    scores = scores * BR + jnp.arange(BR, dtype=jnp.int32)
    order = jnp.argsort(scores, axis=-1)
    return order[:, :, :P_SIZE].astype(jnp.int32)


def plant(entries, rng, smallest, largest):
    longest = entries.shape.index(max(entries.shape))
    spots = []
    for shift in (0, 1):
        where = [jax.random.randint(jax.random.fold_in(rng, axis), (), 0, length) for axis, length in enumerate(entries.shape)]
        where[longest] = (where[longest] + shift) % entries.shape[longest]
        spots.append(tuple(where))
    return entries.at[spots[0]].set(smallest).at[spots[1]].set(largest)


def steps_of(stream_key, dims, split, least, largest):
    def one(position, blocks):
        heights = jax.random.uniform(jax.random.fold_in(jax.random.fold_in(stream_key, 6), position), (blocks,), jnp.float32, least / len(split), largest / len(split))
        return jnp.repeat(jnp.exp(heights), dims[position] // blocks).reshape((-1,) + (1,) * (len(dims) - position - 1))

    factor_of = one(*split[0])
    for cut in split[1:]:
        factor_of = factor_of * one(*cut)
    return factor_of


def noise(own_key, shape, spread, reach, cuts=(), kind=jnp.bfloat16):
    factor_of = steps_of(own_key, shape, cuts, -0.22, 0.18) if cuts else 1.0
    array = jax.random.normal(own_key, shape, jnp.float32) * spread * factor_of
    return jnp.minimum(jnp.maximum(array, -reach), reach).astype(kind)


def setup_inputs(seed: int = 0) -> dict:
    streams_of = jax.random.split(jax.random.key(seed), 5)
    density_blocks = noise(streams_of[0], (N_ROW, NBLK, BLOCK, P_SIZE * BLOCK), (max(BLOCK * N_ROW // (4 * BR), 2)) ** -0.5, 1.0, ((0, 4), (1, 8)))
    density_columns = draw_density_columns(jax.random.fold_in(streams_of[4], 71), 0)
    square_pattern = plant(jax.random.randint(streams_of[2], (N_ROW, NBLK, Q), 0, BR), jax.random.fold_in(streams_of[2], 1), 0, BR - 1).astype(jnp.int32)
    cube_pattern = plant(jax.random.randint(streams_of[3], (N_ROW, NBLK, Q), 0, BR), jax.random.fold_in(streams_of[3], 1), 0, BR - 1).astype(jnp.int32)
    return dict(density_blocks=density_blocks, density_columns=density_columns, square_pattern=square_pattern, cube_pattern=cube_pattern)


def densify(blocks, columns):
    tile_count, row_count, block_size, width = blocks.shape
    slot_count = width // block_size
    tile_ids = jnp.arange(tile_count, dtype=jnp.int32)[:, None, None]
    block_rows = jnp.broadcast_to(jnp.arange(row_count, dtype=jnp.int32)[None, :, None], columns.shape)
    global_cols = (tile_ids * BR + columns).astype(jnp.int32)
    pieces = blocks.astype(jnp.float32).reshape(tile_count, row_count, block_size, slot_count, block_size)
    pieces = jnp.transpose(pieces, (0, 1, 3, 2, 4))
    dense = jnp.zeros((row_count, block_size, tile_count * BR, block_size), jnp.float32)
    dense = dense.at[block_rows, :, global_cols, :].add(pieces)
    return dense.reshape(row_count * block_size, tile_count * BR * block_size)


def extract(dense, columns, block_size):
    tile_count, row_count, slot_count = columns.shape
    grid = dense.reshape(row_count, block_size, tile_count * BR, block_size)
    tile_ids = jnp.arange(tile_count, dtype=jnp.int32)[:, None, None]
    block_rows = jnp.broadcast_to(jnp.arange(row_count, dtype=jnp.int32)[None, :, None], columns.shape)
    global_cols = (tile_ids * BR + columns).astype(jnp.int32)
    pieces = grid[block_rows, :, global_cols, :]
    pieces = jnp.transpose(pieces, (0, 1, 3, 2, 4))
    return pieces.reshape(tile_count, row_count, block_size, slot_count * block_size)


def multiply(first, second):
    return jnp.dot(first, second, precision=lax.Precision.HIGHEST, preferred_element_type=jnp.float32)


def carry_over(second_power, square_pattern, cube_pattern):
    tile_count, row_count, block_size, width = second_power.shape
    slot_count = width // block_size
    matching = (square_pattern[:, :, None, :] == cube_pattern[:, :, :, None]).astype(jnp.float32)
    split_two = second_power.astype(jnp.float32).reshape(tile_count, row_count, block_size, slot_count, block_size)
    carried = jnp.einsum("jgtu,jgxuy->jgxty", matching, split_two, precision=lax.Precision.HIGHEST)
    return carried.reshape(tile_count, row_count, block_size, cube_pattern.shape[2] * block_size)


def reference(density_blocks, density_columns, square_pattern, cube_pattern):
    block_size = density_blocks.shape[2]
    dense_x = densify(density_blocks, density_columns)
    square = multiply(dense_x, dense_x)
    second_power = extract(square, square_pattern, block_size).astype(jnp.bfloat16)
    dense_two = densify(second_power, square_pattern)
    third_power = extract(multiply(dense_two, dense_x), cube_pattern, block_size)
    carried = carry_over(second_power, square_pattern, cube_pattern)
    return 3.0 * carried - 2.0 * third_power
```

```python
import functools

import jax
import jax.numpy as jnp
from jax import lax
from jax.experimental import pallas as pl
from jax.experimental.pallas import tpu as pltpu
from jax.sharding import PartitionSpec as P

MESH = pl.DeviceIdType.MESH
LANES = 128


def kernel(
    sizes, idx_ref, x_ref, out_ref, row_x, row_x2, col_x, chosen, second, idx_vmem_row, idx_vmem_col,
    idx_row, idx_col, row_send, row_recv, x2_send, x2_recv, col_send, col_recv, fwd_send, fwd_recv,
    irow_send, irow_recv, icol_send, icol_recv, local_sem,
):
    n_row, n_col, n_rep, rows, size, slots, q_slots, tile_rows = sizes
    n_chip = n_col // 2
    n_plane = n_col * n_rep
    r, c, p = lax.axis_index("row"), lax.axis_index("col"), lax.axis_index("rep")
    chip, core = c // 2, c % 2
    mine = c * n_rep + p

    def place(k):
        return pl.ds(k * rows, rows)

    own_row = pltpu.make_async_copy(x_ref, row_x.at[r], local_sem.at[0])
    own_row.start()
    own_col = pltpu.make_async_copy(x_ref, col_x.at[place(mine)], local_sem.at[1])
    own_col.start()
    own_irow = pltpu.make_async_copy(idx_ref, idx_vmem_row.at[r], local_sem.at[2])
    own_irow.start()
    own_icol = pltpu.make_async_copy(idx_ref, idx_vmem_col.at[mine], local_sem.at[3])
    own_icol.start()

    row_peers = [(lax.rem(r + d, n_row), lax.rem(r + n_row - d, n_row)) for d in range(1, n_row)]
    plane_peers = []
    for dc in range(n_col):
        for dp in range(n_rep):
            if dc or dp:
                to = (lax.rem(c + dc, n_col), lax.rem(p + dp, n_rep))
                source = lax.rem(c + n_col - dc, n_col) * n_rep + lax.rem(p + n_rep - dp, n_rep)
                plane_peers.append((to, source))
    same_core = []
    for dc in range(n_chip):
        for dp in range(n_rep):
            to = (lax.rem(chip + dc, n_chip) * 2 + core, lax.rem(p + dp, n_rep))
            from_chip = lax.rem(chip + n_chip - dc, n_chip) * 2
            from_rep = lax.rem(p + n_rep - dp, n_rep)
            same_core.append(
                (to, (from_chip + core) * n_rep + from_rep, (from_chip + 1 - core) * n_rep + from_rep)
            )

    barrier = pltpu.get_barrier_semaphore()
    for to, _ in row_peers:
        pl.semaphore_signal(barrier, inc=1, device_id={"row": to}, device_id_type=MESH)
    for (to_c, to_p), _ in plane_peers:
        pl.semaphore_signal(barrier, inc=1, device_id={"col": to_c, "rep": to_p}, device_id_type=MESH)
    pl.semaphore_wait(barrier, len(row_peers) + len(plane_peers))

    def remote(src, dst, send, recv, where):
        return pltpu.make_async_remote_copy(
            src_ref=src, dst_ref=dst, send_sem=send, recv_sem=recv, device_id=where, device_id_type=MESH
        )

    sends = []

    def go(copy):
        copy.start()
        sends.append(copy)

    for i, (to, _) in enumerate(row_peers):
        go(remote(idx_ref, idx_vmem_row.at[r], irow_send.at[i], irow_recv.at[i], {"row": to}))
    for i, ((to_c, to_p), _) in enumerate(plane_peers):
        go(remote(idx_ref, idx_vmem_col.at[mine], icol_send.at[i], icol_recv.at[i], {"col": to_c, "rep": to_p}))
    for i, (to, _) in enumerate(row_peers):
        go(remote(x_ref, row_x.at[r], row_send.at[i], row_recv.at[i], {"row": to}))
    for i, ((to_c, to_p), _, _) in enumerate(same_core):
        if i:
            go(remote(x_ref, col_x.at[place(mine)], col_send.at[i], col_recv.at[i], {"col": to_c, "rep": to_p}))
    sibling = chip * 2 + 1 - core
    go(remote(x_ref, col_x.at[place(mine)], fwd_send.at[0], fwd_recv.at[0], {"col": sibling}))

    own_irow.wait()
    own_icol.wait()
    for i, (to, source) in enumerate(row_peers):
        remote(idx_ref, idx_vmem_row.at[source], irow_send.at[i], irow_recv.at[i], {"row": to}).wait_recv()
    for i, ((to_c, to_p), source) in enumerate(plane_peers):
        remote(
            idx_ref, idx_vmem_col.at[source], icol_send.at[i], icol_recv.at[i], {"col": to_c, "rep": to_p}
        ).wait_recv()
    to_smem_row = pltpu.make_async_copy(idx_vmem_row, idx_row, local_sem.at[4])
    to_smem_row.start()
    to_smem_col = pltpu.make_async_copy(idx_vmem_col, idx_col, local_sem.at[5])
    to_smem_col.start()
    to_smem_row.wait()
    to_smem_col.wait()

    for i, ((to_c, to_p), source, _) in enumerate(same_core):
        if i:
            slab = col_x.at[place(source)]
            remote(x_ref, slab, col_send.at[i], col_recv.at[i], {"col": to_c, "rep": to_p}).wait_recv()
            go(remote(slab, slab, fwd_send.at[i], fwd_recv.at[i], {"col": sibling}))
    own_col.wait()
    for i, (_, _, source) in enumerate(same_core):
        slab = col_x.at[place(source)]
        remote(slab, slab, fwd_send.at[i], fwd_recv.at[i], {"col": sibling}).wait_recv()

    square_at = rows * slots
    cube_at = square_at + rows * q_slots

    def choose(g, j, left_at, left_slots, target_at):
        none = jnp.zeros((size, size), col_x.dtype)
        for t in range(q_slots):
            s = idx_row[r, 0, target_at + g * q_slots + t]
            found = []
            for b in range(tile_rows):
                h = j * tile_rows + b
                block = none
                for q in range(slots):
                    hit = idx_col[h // rows, 0, (h % rows) * slots + q] == s
                    block = lax.select(hit, col_x[h, :, q * size:(q + 1) * size], block)
                found.append(block)
            for u in range(left_slots):
                row = idx_row[j, 0, left_at + g * left_slots + u]
                pick = none
                for b in range(tile_rows):
                    pick = lax.select(row == b, found[b], pick)
                chosen[j, g, u * size:(u + 1) * size, t * size:(t + 1) * size] = pick

    def times(left, j, g, depth):
        return jnp.dot(left, chosen[j, g, :depth], preferred_element_type=jnp.float32)

    for g in range(rows):
        for j in range(n_row):
            choose(g, j, 0, slots, square_at)
    own_row.wait()
    totals = [times(row_x[r, g], r, g, slots * size) for g in range(rows)]
    for i, (to, source) in enumerate(row_peers):
        remote(x_ref, row_x.at[source], row_send.at[i], row_recv.at[i], {"row": to}).wait_recv()
        if i < len(row_peers) - 1:
            for g in range(rows):
                totals[g] += times(row_x[source, g], source, g, slots * size)
    last = row_peers[-1][1]
    for g in range(rows):
        second[g] = (totals[g] + times(row_x[last, g], last, g, slots * size)).astype(second.dtype)
        for i, (to, _) in enumerate(row_peers):
            go(remote(second.at[g], row_x2.at[r, g], x2_send.at[i, g], x2_recv.at[i, g], {"row": to}))

    for g in range(rows):
        for j in range(n_row):
            choose(g, j, square_at, q_slots, cube_at)
    for g in range(rows):
        for t in range(q_slots):
            carried = jnp.zeros((size, size), jnp.float32)
            target = idx_row[r, 0, cube_at + g * q_slots + t]
            for u in range(q_slots):
                weight = jnp.where(idx_row[r, 0, square_at + g * q_slots + u] == target, 3.0, 0.0)
                carried += weight * second[g, :, u * size:(u + 1) * size].astype(jnp.float32)
            out_ref[0, g, :, t * size:(t + 1) * size] = carried
    for g in range(rows):
        total = times(second[g], r, g, q_slots * size)
        for i, (to, source) in enumerate(row_peers):
            remote(
                second.at[g], row_x2.at[source, g], x2_send.at[i, g], x2_recv.at[i, g], {"row": to}
            ).wait_recv()
            total += times(row_x2[source, g], source, g, q_slots * size)
        out_ref[0, g] += -2.0 * total
    for copy in sends:
        copy.wait_send()


def solution(mesh):
    n_row, n_col, n_rep = (mesh.shape[a] for a in ("row", "col", "rep"))

    def on_device(blocks, columns, square_pattern, cube_pattern):
        _, rows, size, width = blocks.shape
        slots, q_slots = columns.shape[2], square_pattern.shape[2]
        n_plane = n_col * n_rep
        n_blocks = n_plane * rows
        tile_rows = n_blocks // n_row
        flat = jnp.concatenate([a.reshape(1, -1) for a in (columns, square_pattern, cube_pattern)], axis=1)
        idx = jnp.pad(flat, ((0, 0), (0, LANES - flat.shape[1])))
        dma = pltpu.SemaphoreType.DMA
        n_same = n_plane // 2
        depth = max(slots, q_slots) * size
        return pl.pallas_call(
            functools.partial(kernel, (n_row, n_col, n_rep, rows, size, slots, q_slots, tile_rows)),
            out_shape=jax.ShapeDtypeStruct((1, rows, size, q_slots * size), jnp.float32),
            in_specs=[pl.BlockSpec(memory_space=pltpu.VMEM), pl.BlockSpec(memory_space=pl.ANY)],
            out_specs=pl.BlockSpec(memory_space=pltpu.VMEM),
            scratch_shapes=[
                pltpu.VMEM((n_row, rows, size, width), blocks.dtype),
                pltpu.VMEM((n_row, rows, size, q_slots * size), blocks.dtype),
                pltpu.VMEM((n_blocks, size, width), blocks.dtype),
                pltpu.VMEM((n_row, rows, depth, q_slots * size), blocks.dtype),
                pltpu.VMEM((rows, size, q_slots * size), blocks.dtype),
                pltpu.VMEM((n_row, 1, LANES), jnp.int32),
                pltpu.VMEM((n_plane, 1, LANES), jnp.int32),
                pltpu.SMEM((n_row, 1, LANES), jnp.int32),
                pltpu.SMEM((n_plane, 1, LANES), jnp.int32),
                dma((n_row,)), dma((n_row,)),
                dma((n_row, rows)), dma((n_row, rows)),
                dma((n_same,)), dma((n_same,)),
                dma((n_same,)), dma((n_same,)),
                dma((n_row,)), dma((n_row,)),
                dma((n_plane,)), dma((n_plane,)),
                dma((6,)),
            ],
            compiler_params=pltpu.CompilerParams(
                collective_id=0, has_side_effects=True, vmem_limit_bytes=40 * 2**20
            ),
        )(idx, blocks[0])

    return jax.shard_map(
        on_device,
        mesh=mesh,
        in_specs=(
            P("row", ("col", "rep"), None, None),
            P("row", ("col", "rep"), None),
            P("row", ("col", "rep"), None),
            P("row", ("col", "rep"), None),
        ),
        out_specs=P("row", ("col", "rep"), None, None),
        check_vma=False,
    )
```

```python
import functools

import jax
import jax.numpy as jnp
from jax import lax
from jax.experimental import pallas as pl
from jax.experimental.pallas import tpu as pltpu
from jax.sharding import PartitionSpec as P

MESH = pl.DeviceIdType.MESH


def kernel(
    sizes, dc_ref, sq_ref, cu_ref, x_ref, out_ref, row_x, row_x2, col_x, chosen, second, dc_row_v, sq_row_v, dc_col_v,
    dc_row, sq_row, dc_col, cube, row_send, row_recv, x2_send, x2_recv, col_send, col_recv, fwd_send, fwd_recv,
    irow_send, irow_recv, icol_send, icol_recv, local_sem,
):
    n_row, n_col, n_rep, rows, size, slots, q_slots, tile_rows = sizes
    n_chip = n_col // 2
    n_plane = n_col * n_rep
    r, c, p = lax.axis_index("row"), lax.axis_index("col"), lax.axis_index("rep")
    chip, core = c // 2, c % 2
    mine = c * n_rep + p

    def place(k):
        return pl.ds(k * rows, rows)

    own_row = pltpu.make_async_copy(x_ref, row_x.at[r], local_sem.at[0])
    own_row.start()
    own_col = pltpu.make_async_copy(x_ref, col_x.at[place(mine)], local_sem.at[1])
    own_col.start()
    own_ints = [
        pltpu.make_async_copy(dc_ref, dc_row_v.at[r], local_sem.at[2]),
        pltpu.make_async_copy(sq_ref, sq_row_v.at[r], local_sem.at[3]),
        pltpu.make_async_copy(dc_ref, dc_col_v.at[mine], local_sem.at[4]),
    ]
    own_cube = pltpu.make_async_copy(cu_ref, cube, local_sem.at[5])
    for copy in (*own_ints, own_cube):
        copy.start()

    row_peers = [(lax.rem(r + d, n_row), lax.rem(r + n_row - d, n_row)) for d in range(1, n_row)]
    plane_peers = []
    for dc in range(n_col):
        for dp in range(n_rep):
            if dc or dp:
                to = (lax.rem(c + dc, n_col), lax.rem(p + dp, n_rep))
                source = lax.rem(c + n_col - dc, n_col) * n_rep + lax.rem(p + n_rep - dp, n_rep)
                plane_peers.append((to, source))
    same_core = []
    for dc in range(n_chip):
        for dp in range(n_rep):
            to = (lax.rem(chip + dc, n_chip) * 2 + core, lax.rem(p + dp, n_rep))
            from_chip = lax.rem(chip + n_chip - dc, n_chip) * 2
            from_rep = lax.rem(p + n_rep - dp, n_rep)
            same_core.append(
                (to, (from_chip + core) * n_rep + from_rep, (from_chip + 1 - core) * n_rep + from_rep)
            )

    barrier = pltpu.get_barrier_semaphore()
    for to, _ in row_peers:
        pl.semaphore_signal(barrier, inc=1, device_id={"row": to}, device_id_type=MESH)
    for (to_c, to_p), _ in plane_peers:
        pl.semaphore_signal(barrier, inc=1, device_id={"col": to_c, "rep": to_p}, device_id_type=MESH)
    pl.semaphore_wait(barrier, len(row_peers) + len(plane_peers))

    def remote(src, dst, send, recv, where):
        return pltpu.make_async_remote_copy(
            src_ref=src, dst_ref=dst, send_sem=send, recv_sem=recv, device_id=where, device_id_type=MESH
        )

    sends = []

    def go(copy):
        copy.start()
        sends.append(copy)

    for i, ((to_c, to_p), _) in enumerate(plane_peers):
        go(remote(dc_ref, dc_col_v.at[mine], icol_send.at[i], icol_recv.at[i], {"col": to_c, "rep": to_p}))
    for i, (to, _) in enumerate(row_peers):
        go(remote(dc_ref, dc_row_v.at[r], irow_send.at[i, 0], irow_recv.at[i, 0], {"row": to}))
        go(remote(sq_ref, sq_row_v.at[r], irow_send.at[i, 1], irow_recv.at[i, 1], {"row": to}))
    for i, (to, _) in enumerate(row_peers):
        go(remote(x_ref.at[0], row_x.at[r, 0], row_send.at[i, 0], row_recv.at[i, 0], {"row": to}))
    sibling = chip * 2 + 1 - core
    for i, ((to_c, to_p), _, _) in enumerate(same_core):
        if i:
            go(remote(x_ref, col_x.at[place(mine)], col_send.at[i], col_recv.at[i], {"col": to_c, "rep": to_p}))
    go(remote(x_ref, col_x.at[place(mine)], fwd_send.at[0], fwd_recv.at[0], {"col": sibling}))
    for g in range(1, rows):
        for i, (to, _) in enumerate(row_peers):
            go(remote(x_ref.at[g], row_x.at[r, g], row_send.at[i, g], row_recv.at[i, g], {"row": to}))

    for copy in own_ints:
        copy.wait()
    for i, ((to_c, to_p), source) in enumerate(plane_peers):
        remote(
            dc_ref, dc_col_v.at[source], icol_send.at[i], icol_recv.at[i], {"col": to_c, "rep": to_p}
        ).wait_recv()
    for i, (to, source) in enumerate(row_peers):
        remote(dc_ref, dc_row_v.at[source], irow_send.at[i, 0], irow_recv.at[i, 0], {"row": to}).wait_recv()
        remote(sq_ref, sq_row_v.at[source], irow_send.at[i, 1], irow_recv.at[i, 1], {"row": to}).wait_recv()
    to_smem = [
        pltpu.make_async_copy(dc_row_v, dc_row, local_sem.at[2]),
        pltpu.make_async_copy(sq_row_v, sq_row, local_sem.at[3]),
        pltpu.make_async_copy(dc_col_v, dc_col, local_sem.at[4]),
    ]
    for copy in to_smem:
        copy.start()

    for i, ((to_c, to_p), source, _) in enumerate(same_core):
        if i:
            slab = col_x.at[place(source)]
            remote(x_ref, slab, col_send.at[i], col_recv.at[i], {"col": to_c, "rep": to_p}).wait_recv()
            go(remote(slab, slab, fwd_send.at[i], fwd_recv.at[i], {"col": sibling}))
    own_col.wait()
    for i, (_, _, source) in enumerate(same_core):
        slab = col_x.at[place(source)]
        remote(slab, slab, fwd_send.at[i], fwd_recv.at[i], {"col": sibling}).wait_recv()

    for copy in to_smem:
        copy.wait()
    own_cube.wait()

    def choose(g, j, left, left_slots, target):
        none = jnp.zeros((size, size), col_x.dtype)
        for t in range(q_slots):
            s = target(g, t)
            found = []
            for b in range(tile_rows):
                h = j * tile_rows + b
                block = none
                for q in range(slots):
                    hit = dc_col[h // rows, h % rows, q] == s
                    block = lax.select(hit, col_x[h, :, q * size:(q + 1) * size], block)
                found.append(block)
            for u in range(left_slots):
                row = left[j, g, u]
                pick = none
                for b in range(tile_rows):
                    pick = lax.select(row == b, found[b], pick)
                chosen[j, g, u * size:(u + 1) * size, t * size:(t + 1) * size] = pick

    def times(left, j, g, depth):
        return jnp.dot(left, chosen[j, g, :depth], preferred_element_type=jnp.float32)

    def square_target(g, t):
        return sq_row[r, g, t]

    def cube_target(g, t):
        return cube[g, t]

    for g in range(rows):
        for j in range(n_row):
            choose(g, j, dc_row, slots, square_target)
    own_row.wait()
    for g in range(rows):
        total = times(row_x[r, g], r, g, slots * size)
        for i, (to, source) in enumerate(row_peers):
            remote(x_ref.at[g], row_x.at[source, g], row_send.at[i, g], row_recv.at[i, g], {"row": to}).wait_recv()
            total += times(row_x[source, g], source, g, slots * size)
        second[g] = total.astype(second.dtype)
        for i, (to, _) in enumerate(row_peers):
            go(remote(second.at[g], row_x2.at[r, g], x2_send.at[i, g], x2_recv.at[i, g], {"row": to}))
        for j in range(n_row):
            choose(g, j, sq_row, q_slots, cube_target)
        for t in range(q_slots):
            carried = jnp.zeros((size, size), jnp.float32)
            for u in range(q_slots):
                weight = jnp.where(sq_row[r, g, u] == cube[g, t], 3.0, 0.0)
                carried += weight * second[g, :, u * size:(u + 1) * size].astype(jnp.float32)
            out_ref[0, g, :, t * size:(t + 1) * size] = carried
    for g in range(rows):
        total = times(second[g], r, g, q_slots * size)
        for i, (to, source) in enumerate(row_peers):
            remote(
                second.at[g], row_x2.at[source, g], x2_send.at[i, g], x2_recv.at[i, g], {"row": to}
            ).wait_recv()
            total += times(row_x2[source, g], source, g, q_slots * size)
        out_ref[0, g] += -2.0 * total
    for copy in sends:
        copy.wait_send()


def solution(mesh):
    n_row, n_col, n_rep = (mesh.shape[a] for a in ("row", "col", "rep"))

    def on_device(blocks, columns, square_pattern, cube_pattern):
        _, rows, size, width = blocks.shape
        slots, q_slots = columns.shape[2], square_pattern.shape[2]
        n_plane = n_col * n_rep
        n_blocks = n_plane * rows
        tile_rows = n_blocks // n_row
        dma = pltpu.SemaphoreType.DMA
        n_same = n_plane // 2
        depth = max(slots, q_slots) * size
        return pl.pallas_call(
            functools.partial(kernel, (n_row, n_col, n_rep, rows, size, slots, q_slots, tile_rows)),
            out_shape=jax.ShapeDtypeStruct((1, rows, size, q_slots * size), jnp.float32),
            in_specs=[pl.BlockSpec(memory_space=pl.ANY)] * 4,
            out_specs=pl.BlockSpec(memory_space=pltpu.VMEM),
            scratch_shapes=[
                pltpu.VMEM((n_row, rows, size, width), blocks.dtype),
                pltpu.VMEM((n_row, rows, size, q_slots * size), blocks.dtype),
                pltpu.VMEM((n_blocks, size, width), blocks.dtype),
                pltpu.VMEM((n_row, rows, depth, q_slots * size), blocks.dtype),
                pltpu.VMEM((rows, size, q_slots * size), blocks.dtype),
                pltpu.VMEM((n_row, rows, slots), jnp.int32),
                pltpu.VMEM((n_row, rows, q_slots), jnp.int32),
                pltpu.VMEM((n_plane, rows, slots), jnp.int32),
                pltpu.SMEM((n_row, rows, slots), jnp.int32),
                pltpu.SMEM((n_row, rows, q_slots), jnp.int32),
                pltpu.SMEM((n_plane, rows, slots), jnp.int32),
                pltpu.SMEM((rows, q_slots), jnp.int32),
                dma((n_row, rows)), dma((n_row, rows)),
                dma((n_row, rows)), dma((n_row, rows)),
                dma((n_same,)), dma((n_same,)),
                dma((n_same,)), dma((n_same,)),
                dma((n_row, 2)), dma((n_row, 2)),
                dma((n_plane,)), dma((n_plane,)),
                dma((6,)),
            ],
            compiler_params=pltpu.CompilerParams(
                collective_id=0, has_side_effects=True, vmem_limit_bytes=60 * 2**20
            ),
        )(columns[0], square_pattern[0], cube_pattern[0], blocks[0])

    return jax.shard_map(
        on_device,
        mesh=mesh,
        in_specs=(
            P("row", ("col", "rep"), None, None),
            P("row", ("col", "rep"), None),
            P("row", ("col", "rep"), None),
            P("row", ("col", "rep"), None),
        ),
        out_specs=P("row", ("col", "rep"), None, None),
        check_vma=False,
    )
```

```python
import functools

import jax
import jax.numpy as jnp
from jax import lax
from jax.experimental import pallas as pl
from jax.experimental.pallas import tpu as pltpu
from jax.sharding import PartitionSpec as P

MESH = pl.DeviceIdType.MESH


def kernel(
    sizes, dc_ref, sq_ref, cu_ref, x_ref, out_ref, row_x, row_x2, col_x, chosen, second, dc_row_v, sq_row_v, dc_col_v,
    dc_row, sq_row, dc_col, cube, row_send, row_recv, x2_send, x2_recv, col_send, col_recv, fwd_send, fwd_recv,
    irow_send, irow_recv, icol_send, icol_recv, local_sem,
):
    n_row, n_col, n_rep, rows, size, slots, q_slots, tile_rows = sizes
    n_chip = n_col // 2
    n_plane = n_col * n_rep
    r, c, p = lax.axis_index("row"), lax.axis_index("col"), lax.axis_index("rep")
    chip, core = c // 2, c % 2
    mine = c * n_rep + p

    def place(k):
        return pl.ds(k * rows, rows)

    own_row = pltpu.make_async_copy(x_ref, row_x.at[r], local_sem.at[0])
    own_row.start()
    own_col = pltpu.make_async_copy(x_ref, col_x.at[place(mine)], local_sem.at[1])
    own_col.start()
    own_ints = [
        pltpu.make_async_copy(dc_ref, dc_row_v.at[r], local_sem.at[2]),
        pltpu.make_async_copy(sq_ref, sq_row_v.at[r], local_sem.at[3]),
        pltpu.make_async_copy(dc_ref, dc_col_v.at[mine], local_sem.at[4]),
    ]
    own_cube = pltpu.make_async_copy(cu_ref, cube, local_sem.at[5])
    for copy in (*own_ints, own_cube):
        copy.start()

    row_peers = [(lax.rem(r + d, n_row), lax.rem(r + n_row - d, n_row)) for d in range(1, n_row)]
    plane_peers = []
    for dc in range(n_col):
        for dp in range(n_rep):
            if dc or dp:
                to = (lax.rem(c + dc, n_col), lax.rem(p + dp, n_rep))
                source = lax.rem(c + n_col - dc, n_col) * n_rep + lax.rem(p + n_rep - dp, n_rep)
                plane_peers.append((to, source))
    same_core = []
    for dc in range(n_chip):
        for dp in range(n_rep):
            to = (lax.rem(chip + dc, n_chip) * 2 + core, lax.rem(p + dp, n_rep))
            from_chip = lax.rem(chip + n_chip - dc, n_chip) * 2
            from_rep = lax.rem(p + n_rep - dp, n_rep)
            same_core.append(
                (to, (from_chip + core) * n_rep + from_rep, (from_chip + 1 - core) * n_rep + from_rep)
            )

    barrier = pltpu.get_barrier_semaphore()
    for to, _ in row_peers:
        pl.semaphore_signal(barrier, inc=1, device_id={"row": to}, device_id_type=MESH)
    for (to_c, to_p), _ in plane_peers:
        pl.semaphore_signal(barrier, inc=1, device_id={"col": to_c, "rep": to_p}, device_id_type=MESH)
    pl.semaphore_wait(barrier, len(row_peers) + len(plane_peers))

    def remote(src, dst, send, recv, where):
        return pltpu.make_async_remote_copy(
            src_ref=src, dst_ref=dst, send_sem=send, recv_sem=recv, device_id=where, device_id_type=MESH
        )

    sends = []

    def go(copy):
        copy.start()
        sends.append(copy)

    for i, ((to_c, to_p), _) in enumerate(plane_peers):
        go(remote(dc_ref, dc_col_v.at[mine], icol_send.at[i], icol_recv.at[i], {"col": to_c, "rep": to_p}))
    for i, (to, _) in enumerate(row_peers):
        go(remote(dc_ref, dc_row_v.at[r], irow_send.at[i, 0], irow_recv.at[i, 0], {"row": to}))
        go(remote(sq_ref, sq_row_v.at[r], irow_send.at[i, 1], irow_recv.at[i, 1], {"row": to}))
    for i, (to, _) in enumerate(row_peers):
        go(remote(x_ref.at[0], row_x.at[r, 0], row_send.at[i, 0], row_recv.at[i, 0], {"row": to}))
    sibling = chip * 2 + 1 - core
    for i, ((to_c, to_p), _, _) in enumerate(same_core):
        if i:
            go(remote(x_ref, col_x.at[place(mine)], col_send.at[i], col_recv.at[i], {"col": to_c, "rep": to_p}))
    go(remote(x_ref, col_x.at[place(mine)], fwd_send.at[0], fwd_recv.at[0], {"col": sibling}))
    for g in range(1, rows):
        for i, (to, _) in enumerate(row_peers):
            go(remote(x_ref.at[g], row_x.at[r, g], row_send.at[i, g], row_recv.at[i, g], {"row": to}))

    for i, ((to_c, to_p), source, _) in enumerate(same_core):
        if i:
            slab = col_x.at[place(source)]
            remote(x_ref, slab, col_send.at[i], col_recv.at[i], {"col": to_c, "rep": to_p}).wait_recv()
            go(remote(slab, slab, fwd_send.at[i], fwd_recv.at[i], {"col": sibling}))
    for copy in own_ints:
        copy.wait()
    for i, ((to_c, to_p), source) in enumerate(plane_peers):
        remote(
            dc_ref, dc_col_v.at[source], icol_send.at[i], icol_recv.at[i], {"col": to_c, "rep": to_p}
        ).wait_recv()
    for i, (to, source) in enumerate(row_peers):
        remote(dc_ref, dc_row_v.at[source], irow_send.at[i, 0], irow_recv.at[i, 0], {"row": to}).wait_recv()
        remote(sq_ref, sq_row_v.at[source], irow_send.at[i, 1], irow_recv.at[i, 1], {"row": to}).wait_recv()
    to_smem = [
        pltpu.make_async_copy(dc_row_v, dc_row, local_sem.at[2]),
        pltpu.make_async_copy(sq_row_v, sq_row, local_sem.at[3]),
        pltpu.make_async_copy(dc_col_v, dc_col, local_sem.at[4]),
    ]
    for copy in to_smem:
        copy.start()

    own_col.wait()
    for i, (_, _, source) in enumerate(same_core):
        slab = col_x.at[place(source)]
        remote(slab, slab, fwd_send.at[i], fwd_recv.at[i], {"col": sibling}).wait_recv()

    for copy in to_smem:
        copy.wait()
    own_cube.wait()

    def choose(g, j, left, left_slots, target):
        none = jnp.zeros((size, size), col_x.dtype)
        for t in range(q_slots):
            s = target(g, t)
            found = []
            for b in range(tile_rows):
                h = j * tile_rows + b
                block = none
                for q in range(slots):
                    hit = dc_col[h // rows, h % rows, q] == s
                    block = lax.select(hit, col_x[h, :, q * size:(q + 1) * size], block)
                found.append(block)
            for u in range(left_slots):
                row = left[j, g, u]
                pick = none
                for b in range(tile_rows):
                    pick = lax.select(row == b, found[b], pick)
                chosen[j, g, u * size:(u + 1) * size, t * size:(t + 1) * size] = pick

    def times(left, j, g, depth):
        return jnp.dot(left, chosen[j, g, :depth], preferred_element_type=jnp.float32)

    def square_target(g, t):
        return sq_row[r, g, t]

    def cube_target(g, t):
        return cube[g, t]

    own_row.wait()
    for g in range(rows):
        for j in range(n_row):
            choose(g, j, dc_row, slots, square_target)
        total = times(row_x[r, g], r, g, slots * size)
        for i, (to, source) in enumerate(row_peers):
            remote(x_ref.at[g], row_x.at[source, g], row_send.at[i, g], row_recv.at[i, g], {"row": to}).wait_recv()
            total += times(row_x[source, g], source, g, slots * size)
        second[g] = total.astype(second.dtype)
        for i, (to, _) in enumerate(row_peers):
            go(remote(second.at[g], row_x2.at[r, g], x2_send.at[i, g], x2_recv.at[i, g], {"row": to}))
    for g in range(rows):
        for j in range(n_row):
            choose(g, j, sq_row, q_slots, cube_target)
        for t in range(q_slots):
            carried = jnp.zeros((size, size), jnp.float32)
            for u in range(q_slots):
                weight = jnp.where(sq_row[r, g, u] == cube[g, t], 3.0, 0.0)
                carried += weight * second[g, :, u * size:(u + 1) * size].astype(jnp.float32)
            out_ref[0, g, :, t * size:(t + 1) * size] = carried
    for g in range(rows):
        total = times(second[g], r, g, q_slots * size)
        for i, (to, source) in enumerate(row_peers):
            remote(
                second.at[g], row_x2.at[source, g], x2_send.at[i, g], x2_recv.at[i, g], {"row": to}
            ).wait_recv()
            total += times(row_x2[source, g], source, g, q_slots * size)
        out_ref[0, g] += -2.0 * total
    for copy in sends:
        copy.wait_send()


def solution(mesh):
    n_row, n_col, n_rep = (mesh.shape[a] for a in ("row", "col", "rep"))

    def on_device(blocks, columns, square_pattern, cube_pattern):
        _, rows, size, width = blocks.shape
        slots, q_slots = columns.shape[2], square_pattern.shape[2]
        n_plane = n_col * n_rep
        n_blocks = n_plane * rows
        tile_rows = n_blocks // n_row
        dma = pltpu.SemaphoreType.DMA
        n_same = n_plane // 2
        depth = max(slots, q_slots) * size
        return pl.pallas_call(
            functools.partial(kernel, (n_row, n_col, n_rep, rows, size, slots, q_slots, tile_rows)),
            out_shape=jax.ShapeDtypeStruct((1, rows, size, q_slots * size), jnp.float32),
            in_specs=[pl.BlockSpec(memory_space=pltpu.HBM)] * 4,
            out_specs=pl.BlockSpec(memory_space=pltpu.VMEM),
            scratch_shapes=[
                pltpu.VMEM((n_row, rows, size, width), blocks.dtype),
                pltpu.VMEM((n_row, rows, size, q_slots * size), blocks.dtype),
                pltpu.VMEM((n_blocks, size, width), blocks.dtype),
                pltpu.VMEM((n_row, rows, depth, q_slots * size), blocks.dtype),
                pltpu.VMEM((rows, size, q_slots * size), blocks.dtype),
                pltpu.VMEM((n_row, rows, slots), jnp.int32),
                pltpu.VMEM((n_row, rows, q_slots), jnp.int32),
                pltpu.VMEM((n_plane, rows, slots), jnp.int32),
                pltpu.SMEM((n_row, rows, slots), jnp.int32),
                pltpu.SMEM((n_row, rows, q_slots), jnp.int32),
                pltpu.SMEM((n_plane, rows, slots), jnp.int32),
                pltpu.SMEM((rows, q_slots), jnp.int32),
                dma((n_row, rows)), dma((n_row, rows)),
                dma((n_row, rows)), dma((n_row, rows)),
                dma((n_same,)), dma((n_same,)),
                dma((n_same,)), dma((n_same,)),
                dma((n_row, 2)), dma((n_row, 2)),
                dma((n_plane,)), dma((n_plane,)),
                dma((6,)),
            ],
            compiler_params=pltpu.CompilerParams(
                collective_id=0, has_side_effects=True, vmem_limit_bytes=32 * 2**20
            ),
        )(columns[0], square_pattern[0], cube_pattern[0], blocks[0])

    return jax.shard_map(
        on_device,
        mesh=mesh,
        in_specs=(
            P("row", ("col", "rep"), None, None),
            P("row", ("col", "rep"), None),
            P("row", ("col", "rep"), None),
            P("row", ("col", "rep"), None),
        ),
        out_specs=P("row", ("col", "rep"), None, None),
        check_vma=False,
    )
```

```python
import functools

import jax
import jax.numpy as jnp
from jax import lax
from jax.experimental import pallas as pl
from jax.experimental.pallas import tpu as pltpu
from jax.sharding import PartitionSpec as P

MESH = pl.DeviceIdType.MESH


def kernel(
    sizes, dc_ref, sq_ref, cu_ref, x_ref, out_ref, row_x, row_x2, col_x, chosen, second, dc_row_v, sq_row_v, dc_col_v,
    dc_row, sq_row, dc_col, cube, row_send, row_recv, x2_send, x2_recv, col_send, col_recv, fwd_send, fwd_recv,
    irow_send, irow_recv, icol_send, icol_recv, local_sem,
):
    n_row, n_col, n_rep, rows, size, slots, q_slots, tile_rows = sizes
    n_chip = n_col // 2
    n_plane = n_col * n_rep
    r, c, p = lax.axis_index("row"), lax.axis_index("col"), lax.axis_index("rep")
    chip, core = c // 2, c % 2
    mine = c * n_rep + p

    def place(k):
        return pl.ds(k * rows, rows)

    own_row = pltpu.make_async_copy(x_ref, row_x.at[r], local_sem.at[0])
    own_row.start()
    own_col = pltpu.make_async_copy(x_ref, col_x.at[place(mine)], local_sem.at[1])
    own_col.start()
    own_ints = [
        pltpu.make_async_copy(dc_ref, dc_row_v.at[r], local_sem.at[2]),
        pltpu.make_async_copy(sq_ref, sq_row_v.at[r], local_sem.at[3]),
        pltpu.make_async_copy(dc_ref, dc_col_v.at[mine], local_sem.at[4]),
    ]
    own_cube = pltpu.make_async_copy(cu_ref, cube, local_sem.at[5])
    for copy in (*own_ints, own_cube):
        copy.start()

    row_peers = [(lax.rem(r + d, n_row), lax.rem(r + n_row - d, n_row)) for d in range(1, n_row)]
    plane_peers = []
    for dc in range(n_col):
        for dp in range(n_rep):
            if dc or dp:
                to = (lax.rem(c + dc, n_col), lax.rem(p + dp, n_rep))
                source = lax.rem(c + n_col - dc, n_col) * n_rep + lax.rem(p + n_rep - dp, n_rep)
                plane_peers.append((to, source))
    same_core = []
    for dc in range(n_chip):
        for dp in range(n_rep):
            to = (lax.rem(chip + dc, n_chip) * 2 + core, lax.rem(p + dp, n_rep))
            from_chip = lax.rem(chip + n_chip - dc, n_chip) * 2
            from_rep = lax.rem(p + n_rep - dp, n_rep)
            same_core.append(
                (to, (from_chip + core) * n_rep + from_rep, (from_chip + 1 - core) * n_rep + from_rep)
            )

    barrier = pltpu.get_barrier_semaphore()
    for to, _ in row_peers:
        pl.semaphore_signal(barrier, inc=1, device_id={"row": to}, device_id_type=MESH)
    for (to_c, to_p), _ in plane_peers:
        pl.semaphore_signal(barrier, inc=1, device_id={"col": to_c, "rep": to_p}, device_id_type=MESH)
    pl.semaphore_wait(barrier, len(row_peers) + len(plane_peers))

    def remote(src, dst, send, recv, where):
        return pltpu.make_async_remote_copy(
            src_ref=src, dst_ref=dst, send_sem=send, recv_sem=recv, device_id=where, device_id_type=MESH
        )

    sends = []

    def go(copy):
        copy.start()
        sends.append(copy)

    sibling = chip * 2 + 1 - core
    for i, ((to_c, to_p), _, _) in enumerate(same_core):
        if i:
            go(remote(x_ref, col_x.at[place(mine)], col_send.at[i], col_recv.at[i], {"col": to_c, "rep": to_p}))
    go(remote(x_ref, col_x.at[place(mine)], fwd_send.at[0], fwd_recv.at[0], {"col": sibling}))
    for i, (to, _) in enumerate(row_peers):
        go(remote(x_ref.at[0], row_x.at[r, 0], row_send.at[i, 0], row_recv.at[i, 0], {"row": to}))
    for i, ((to_c, to_p), _) in enumerate(plane_peers):
        go(remote(dc_ref, dc_col_v.at[mine], icol_send.at[i], icol_recv.at[i], {"col": to_c, "rep": to_p}))
    for i, (to, _) in enumerate(row_peers):
        go(remote(dc_ref, dc_row_v.at[r], irow_send.at[i, 0], irow_recv.at[i, 0], {"row": to}))
        go(remote(sq_ref, sq_row_v.at[r], irow_send.at[i, 1], irow_recv.at[i, 1], {"row": to}))
    for g in range(1, rows):
        for i, (to, _) in enumerate(row_peers):
            go(remote(x_ref.at[g], row_x.at[r, g], row_send.at[i, g], row_recv.at[i, g], {"row": to}))

    for i, ((to_c, to_p), source, _) in enumerate(same_core):
        if i:
            slab = col_x.at[place(source)]
            remote(x_ref, slab, col_send.at[i], col_recv.at[i], {"col": to_c, "rep": to_p}).wait_recv()
            go(remote(slab, slab, fwd_send.at[i], fwd_recv.at[i], {"col": sibling}))
    for copy in own_ints:
        copy.wait()
    for i, ((to_c, to_p), source) in enumerate(plane_peers):
        remote(
            dc_ref, dc_col_v.at[source], icol_send.at[i], icol_recv.at[i], {"col": to_c, "rep": to_p}
        ).wait_recv()
    for i, (to, source) in enumerate(row_peers):
        remote(dc_ref, dc_row_v.at[source], irow_send.at[i, 0], irow_recv.at[i, 0], {"row": to}).wait_recv()
        remote(sq_ref, sq_row_v.at[source], irow_send.at[i, 1], irow_recv.at[i, 1], {"row": to}).wait_recv()
    to_smem = [
        pltpu.make_async_copy(dc_row_v, dc_row, local_sem.at[2]),
        pltpu.make_async_copy(sq_row_v, sq_row, local_sem.at[3]),
        pltpu.make_async_copy(dc_col_v, dc_col, local_sem.at[4]),
    ]
    for copy in to_smem:
        copy.start()

    own_col.wait()
    for i, (_, _, source) in enumerate(same_core):
        slab = col_x.at[place(source)]
        remote(slab, slab, fwd_send.at[i], fwd_recv.at[i], {"col": sibling}).wait_recv()

    for copy in to_smem:
        copy.wait()
    own_cube.wait()

    def choose(g, j, left, left_slots, target):
        none = jnp.zeros((size, size), col_x.dtype)
        for t in range(q_slots):
            s = target(g, t)
            found = []
            for b in range(tile_rows):
                h = j * tile_rows + b
                block = none
                for q in range(slots):
                    hit = dc_col[h // rows, h % rows, q] == s
                    block = lax.select(hit, col_x[h, :, q * size:(q + 1) * size], block)
                found.append(block)
            for u in range(left_slots):
                row = left[j, g, u]
                pick = none
                for b in range(tile_rows):
                    pick = lax.select(row == b, found[b], pick)
                chosen[j, g, u * size:(u + 1) * size, t * size:(t + 1) * size] = pick

    def times(left, j, g, depth):
        return jnp.dot(left, chosen[j, g, :depth], preferred_element_type=jnp.float32)

    def square_target(g, t):
        return sq_row[r, g, t]

    def cube_target(g, t):
        return cube[g, t]

    own_row.wait()
    for g in range(rows):
        for j in range(n_row):
            choose(g, j, dc_row, slots, square_target)
        total = times(row_x[r, g], r, g, slots * size)
        for i, (to, source) in enumerate(row_peers):
            remote(x_ref.at[g], row_x.at[source, g], row_send.at[i, g], row_recv.at[i, g], {"row": to}).wait_recv()
            total += times(row_x[source, g], source, g, slots * size)
        second[g] = total.astype(second.dtype)
        for i, (to, _) in enumerate(row_peers):
            go(remote(second.at[g], row_x2.at[r, g], x2_send.at[i, g], x2_recv.at[i, g], {"row": to}))
    for g in range(rows):
        for j in range(n_row):
            choose(g, j, sq_row, q_slots, cube_target)
        for t in range(q_slots):
            carried = jnp.zeros((size, size), jnp.float32)
            for u in range(q_slots):
                weight = jnp.where(sq_row[r, g, u] == cube[g, t], 3.0, 0.0)
                carried += weight * second[g, :, u * size:(u + 1) * size].astype(jnp.float32)
            out_ref[0, g, :, t * size:(t + 1) * size] = carried
    for g in range(rows):
        total = times(second[g], r, g, q_slots * size)
        for i, (to, source) in enumerate(row_peers):
            remote(
                second.at[g], row_x2.at[source, g], x2_send.at[i, g], x2_recv.at[i, g], {"row": to}
            ).wait_recv()
            total += times(row_x2[source, g], source, g, q_slots * size)
        out_ref[0, g] += -2.0 * total
    for copy in sends:
        copy.wait_send()


def solution(mesh):
    n_row, n_col, n_rep = (mesh.shape[a] for a in ("row", "col", "rep"))

    def on_device(blocks, columns, square_pattern, cube_pattern):
        _, rows, size, width = blocks.shape
        slots, q_slots = columns.shape[2], square_pattern.shape[2]
        n_plane = n_col * n_rep
        n_blocks = n_plane * rows
        tile_rows = n_blocks // n_row
        dma = pltpu.SemaphoreType.DMA
        n_same = n_plane // 2
        depth = max(slots, q_slots) * size
        return pl.pallas_call(
            functools.partial(kernel, (n_row, n_col, n_rep, rows, size, slots, q_slots, tile_rows)),
            out_shape=jax.ShapeDtypeStruct((1, rows, size, q_slots * size), jnp.float32),
            in_specs=[pl.BlockSpec(memory_space=pltpu.HBM)] * 4,
            out_specs=pl.BlockSpec(memory_space=pltpu.VMEM),
            scratch_shapes=[
                pltpu.VMEM((n_row, rows, size, width), blocks.dtype),
                pltpu.VMEM((n_row, rows, size, q_slots * size), blocks.dtype),
                pltpu.VMEM((n_blocks, size, width), blocks.dtype),
                pltpu.VMEM((n_row, rows, depth, q_slots * size), blocks.dtype),
                pltpu.VMEM((rows, size, q_slots * size), blocks.dtype),
                pltpu.VMEM((n_row, rows, slots), jnp.int32),
                pltpu.VMEM((n_row, rows, q_slots), jnp.int32),
                pltpu.VMEM((n_plane, rows, slots), jnp.int32),
                pltpu.SMEM((n_row, rows, slots), jnp.int32),
                pltpu.SMEM((n_row, rows, q_slots), jnp.int32),
                pltpu.SMEM((n_plane, rows, slots), jnp.int32),
                pltpu.SMEM((rows, q_slots), jnp.int32),
                dma((n_row, rows)), dma((n_row, rows)),
                dma((n_row, rows)), dma((n_row, rows)),
                dma((n_same,)), dma((n_same,)),
                dma((n_same,)), dma((n_same,)),
                dma((n_row, 2)), dma((n_row, 2)),
                dma((n_plane,)), dma((n_plane,)),
                dma((6,)),
            ],
            compiler_params=pltpu.CompilerParams(
                collective_id=0, has_side_effects=True, vmem_limit_bytes=32 * 2**20
            ),
        )(columns[0], square_pattern[0], cube_pattern[0], blocks[0])

    return jax.shard_map(
        on_device,
        mesh=mesh,
        in_specs=(
            P("row", ("col", "rep"), None, None),
            P("row", ("col", "rep"), None),
            P("row", ("col", "rep"), None),
            P("row", ("col", "rep"), None),
        ),
        out_specs=P("row", ("col", "rep"), None, None),
        check_vma=False,
    )
```

```python
import functools

import jax
import jax.numpy as jnp
from jax import lax
from jax.experimental import pallas as pl
from jax.experimental.pallas import tpu as pltpu
from jax.sharding import PartitionSpec as P

MESH = pl.DeviceIdType.MESH


def kernel(
    sizes, dc_ref, sq_ref, cu_ref, x_ref, out_ref, row_x, row_x2, col_x, chosen, second, dc_row_v, sq_row_v, dc_col_v,
    dc_row, sq_row, dc_col, cube, row_send, row_recv, x2_send, x2_recv, col_send, col_recv, fwd_send, fwd_recv,
    irow_send, irow_recv, icol_send, icol_recv, local_sem,
):
    n_row, n_col, n_rep, rows, size, slots, q_slots, tile_rows = sizes
    n_chip = n_col // 2
    n_plane = n_col * n_rep
    r, c, p = lax.axis_index("row"), lax.axis_index("col"), lax.axis_index("rep")
    chip, core = c // 2, c % 2
    mine = c * n_rep + p

    def place(k):
        return pl.ds(k * rows, rows)

    own_row = pltpu.make_async_copy(x_ref, row_x.at[r], local_sem.at[0])
    own_row.start()
    own_col = pltpu.make_async_copy(x_ref, col_x.at[place(mine)], local_sem.at[1])
    own_col.start()
    own_ints = [
        pltpu.make_async_copy(dc_ref, dc_row_v.at[r], local_sem.at[2]),
        pltpu.make_async_copy(sq_ref, sq_row_v.at[r], local_sem.at[3]),
        pltpu.make_async_copy(dc_ref, dc_col_v.at[mine], local_sem.at[4]),
    ]
    own_cube = pltpu.make_async_copy(cu_ref, cube, local_sem.at[5])
    for copy in (*own_ints, own_cube):
        copy.start()

    row_peers = [(lax.rem(r + d, n_row), lax.rem(r + n_row - d, n_row)) for d in range(1, n_row)]
    plane_peers = []
    for dc in range(n_col):
        for dp in range(n_rep):
            if dc or dp:
                to = (lax.rem(c + dc, n_col), lax.rem(p + dp, n_rep))
                source = lax.rem(c + n_col - dc, n_col) * n_rep + lax.rem(p + n_rep - dp, n_rep)
                plane_peers.append((to, source))
    same_core = []
    for dc in range(n_chip):
        for dp in range(n_rep):
            to = (lax.rem(chip + dc, n_chip) * 2 + core, lax.rem(p + dp, n_rep))
            from_chip = lax.rem(chip + n_chip - dc, n_chip) * 2
            from_rep = lax.rem(p + n_rep - dp, n_rep)
            same_core.append(
                (to, (from_chip + core) * n_rep + from_rep, (from_chip + 1 - core) * n_rep + from_rep)
            )

    barrier = pltpu.get_barrier_semaphore()
    for to, _ in row_peers:
        pl.semaphore_signal(barrier, inc=1, device_id={"row": to}, device_id_type=MESH)
    for (to_c, to_p), _ in plane_peers:
        pl.semaphore_signal(barrier, inc=1, device_id={"col": to_c, "rep": to_p}, device_id_type=MESH)
    pl.semaphore_wait(barrier, len(row_peers) + len(plane_peers))

    def remote(src, dst, send, recv, where):
        return pltpu.make_async_remote_copy(
            src_ref=src, dst_ref=dst, send_sem=send, recv_sem=recv, device_id=where, device_id_type=MESH
        )

    sends = []

    def go(copy):
        copy.start()
        sends.append(copy)

    for i, ((to_c, to_p), _) in enumerate(plane_peers):
        go(remote(dc_ref, dc_col_v.at[mine], icol_send.at[i], icol_recv.at[i], {"col": to_c, "rep": to_p}))
    for i, (to, _) in enumerate(row_peers):
        go(remote(dc_ref, dc_row_v.at[r], irow_send.at[i, 0], irow_recv.at[i, 0], {"row": to}))
        go(remote(sq_ref, sq_row_v.at[r], irow_send.at[i, 1], irow_recv.at[i, 1], {"row": to}))
    for i, (to, _) in enumerate(row_peers):
        go(remote(x_ref.at[0], row_x.at[r, 0], row_send.at[i, 0], row_recv.at[i, 0], {"row": to}))
    sibling = chip * 2 + 1 - core
    for i, ((to_c, to_p), _, _) in enumerate(same_core):
        if i:
            go(remote(x_ref, col_x.at[place(mine)], col_send.at[i], col_recv.at[i], {"col": to_c, "rep": to_p}))
    go(remote(x_ref, col_x.at[place(mine)], fwd_send.at[0], fwd_recv.at[0], {"col": sibling}))
    for g in range(1, rows):
        for i, (to, _) in enumerate(row_peers):
            go(remote(x_ref.at[g], row_x.at[r, g], row_send.at[i, g], row_recv.at[i, g], {"row": to}))

    for i, ((to_c, to_p), source, _) in enumerate(same_core):
        if i:
            slab = col_x.at[place(source)]
            remote(x_ref, slab, col_send.at[i], col_recv.at[i], {"col": to_c, "rep": to_p}).wait_recv()
            go(remote(slab, slab, fwd_send.at[i], fwd_recv.at[i], {"col": sibling}))
    for copy in own_ints:
        copy.wait()
    for i, ((to_c, to_p), source) in enumerate(plane_peers):
        remote(
            dc_ref, dc_col_v.at[source], icol_send.at[i], icol_recv.at[i], {"col": to_c, "rep": to_p}
        ).wait_recv()
    for i, (to, source) in enumerate(row_peers):
        remote(dc_ref, dc_row_v.at[source], irow_send.at[i, 0], irow_recv.at[i, 0], {"row": to}).wait_recv()
        remote(sq_ref, sq_row_v.at[source], irow_send.at[i, 1], irow_recv.at[i, 1], {"row": to}).wait_recv()
    to_smem = [
        pltpu.make_async_copy(dc_row_v, dc_row, local_sem.at[2]),
        pltpu.make_async_copy(sq_row_v, sq_row, local_sem.at[3]),
        pltpu.make_async_copy(dc_col_v, dc_col, local_sem.at[4]),
    ]
    for copy in to_smem:
        copy.start()

    own_col.wait()
    for i, (_, _, source) in enumerate(same_core):
        slab = col_x.at[place(source)]
        remote(slab, slab, fwd_send.at[i], fwd_recv.at[i], {"col": sibling}).wait_recv()

    for copy in to_smem:
        copy.wait()
    own_cube.wait()

    def choose(g, j, left, left_slots, target):
        none = jnp.zeros((size, size), col_x.dtype)
        for t in range(q_slots):
            s = target(g, t)
            found = []
            for b in range(tile_rows):
                h = j * tile_rows + b
                block = none
                for q in range(slots):
                    hit = dc_col[h // rows, h % rows, q] == s
                    block = lax.select(hit, col_x[h, :, q * size:(q + 1) * size], block)
                found.append(block)
            for u in range(left_slots):
                row = left[j, g, u]
                pick = none
                for b in range(tile_rows):
                    pick = lax.select(row == b, found[b], pick)
                chosen[j, g, u * size:(u + 1) * size, t * size:(t + 1) * size] = pick

    def times(left, j, g, depth):
        return jnp.dot(left, chosen[j, g, :depth], preferred_element_type=jnp.float32)

    def square_target(g, t):
        return sq_row[r, g, t]

    def cube_target(g, t):
        return cube[g, t]

    own_row.wait()
    for g in range(rows):
        for j in range(n_row):
            choose(g, j, dc_row, slots, square_target)
        total = times(row_x[r, g], r, g, slots * size)
        for i, (to, source) in enumerate(row_peers):
            remote(x_ref.at[g], row_x.at[source, g], row_send.at[i, g], row_recv.at[i, g], {"row": to}).wait_recv()
            total += times(row_x[source, g], source, g, slots * size)
        second[g] = total.astype(second.dtype)
        for i, (to, _) in enumerate(row_peers):
            go(remote(second.at[g], row_x2.at[r, g], x2_send.at[i, g], x2_recv.at[i, g], {"row": to}))
    for g in range(rows):
        for j in range(n_row):
            choose(g, j, sq_row, q_slots, cube_target)
        for t in range(q_slots):
            carried = jnp.zeros((size, size), jnp.float32)
            for u in range(q_slots):
                weight = jnp.where(sq_row[r, g, u] == cube[g, t], 3.0, 0.0)
                carried += weight * second[g, :, u * size:(u + 1) * size].astype(jnp.float32)
            out_ref[0, g, :, t * size:(t + 1) * size] = carried
    for g in range(rows):
        total = times(second[g], r, g, q_slots * size)
        for i, (to, source) in enumerate(row_peers):
            remote(
                second.at[g], row_x2.at[source, g], x2_send.at[i, g], x2_recv.at[i, g], {"row": to}
            ).wait_recv()
            total += times(row_x2[source, g], source, g, q_slots * size)
        out_ref[0, g] += -2.0 * total
    for copy in sends:
        copy.wait_send()


def solution(mesh):
    n_row, n_col, n_rep = (mesh.shape[a] for a in ("row", "col", "rep"))

    def on_device(blocks, columns, square_pattern, cube_pattern):
        _, rows, size, width = blocks.shape
        slots, q_slots = columns.shape[2], square_pattern.shape[2]
        n_plane = n_col * n_rep
        n_blocks = n_plane * rows
        tile_rows = n_blocks // n_row
        dma = pltpu.SemaphoreType.DMA
        n_same = n_plane // 2
        depth = max(slots, q_slots) * size
        return pl.pallas_call(
            functools.partial(kernel, (n_row, n_col, n_rep, rows, size, slots, q_slots, tile_rows)),
            out_shape=jax.ShapeDtypeStruct((1, rows, size, q_slots * size), jnp.float32),
            in_specs=[pl.BlockSpec(memory_space=pltpu.HBM)] * 4,
            out_specs=pl.BlockSpec(memory_space=pltpu.VMEM),
            scratch_shapes=[
                pltpu.VMEM((n_row, rows, size, width), blocks.dtype),
                pltpu.VMEM((n_row, rows, size, q_slots * size), blocks.dtype),
                pltpu.VMEM((n_blocks, size, width), blocks.dtype),
                pltpu.VMEM((n_row, rows, depth, q_slots * size), blocks.dtype),
                pltpu.VMEM((rows, size, q_slots * size), blocks.dtype),
                pltpu.VMEM((n_row, rows, slots), jnp.int32),
                pltpu.VMEM((n_row, rows, q_slots), jnp.int32),
                pltpu.VMEM((n_plane, rows, slots), jnp.int32),
                pltpu.SMEM((n_row, rows, slots), jnp.int32),
                pltpu.SMEM((n_row, rows, q_slots), jnp.int32),
                pltpu.SMEM((n_plane, rows, slots), jnp.int32),
                pltpu.SMEM((rows, q_slots), jnp.int32),
                dma((n_row, rows)), dma((n_row, rows)),
                dma((n_row, rows)), dma((n_row, rows)),
                dma((n_same,)), dma((n_same,)),
                dma((n_same,)), dma((n_same,)),
                dma((n_row, 2)), dma((n_row, 2)),
                dma((n_plane,)), dma((n_plane,)),
                dma((6,)),
            ],
            compiler_params=pltpu.CompilerParams(
                collective_id=0, has_side_effects=True, vmem_limit_bytes=60 * 2**20
            ),
        )(columns[0], square_pattern[0], cube_pattern[0], blocks[0])

    return jax.shard_map(
        on_device,
        mesh=mesh,
        in_specs=(
            P("row", ("col", "rep"), None, None),
            P("row", ("col", "rep"), None),
            P("row", ("col", "rep"), None),
            P("row", ("col", "rep"), None),
        ),
        out_specs=P("row", ("col", "rep"), None, None),
        check_vma=False,
    )
```
